32 devices in a mesh: path: 4 (over z), mp: 2 (over core), period: 4 (over y, x).
Axes of the slice: x: 2, y: 2, z: 4, core: 2. Of those that a mesh axis runs over, the one named last changes fastest.
Arguments:
- tiles: bfloat16 [512, 256, 256], P(('path', 'mp')), may hold values from -0.375 to 0.375
- tile_rows: int32 [512], P(('path', 'mp')), may hold values from 0 to 7
- tile_cols: int32 [512], P(('path', 'mp')), may hold values from 0 to 127, as said below
- tile_counts: int32 [8], P(('path', 'mp')), may hold values from 8 to 64, as said below
- data: float32 [32768], P(('period', 'path')), parts along dimension 0, may hold values from -6 to 6
Outputs:
- solution: float32 [262144], P(('period', 'path', 'mp')), parts along dimension 0
- left_vector: float32 [32768], P(('period', 'path')), parts along dimension 0
The draws below stay inside these ranges and needn't reach their ends.
There are 4 independent parts, one for each index of `period`. The reference program is written for one: setup_inputs(seed, part) draws one part's arguments, and reference() takes and returns one part's arrays. A program takes and returns all parts, laid end to end along the dimension named above; an argument that names none is the same for every part. Nothing has to cross between parts.
Inputs may be any that keep to these rules, and one draw needn't show every extreme that they name: `tile_counts`: slots from the strip's count on are unused; some strips are full. `tile_cols`: among all 64 slots of one strip, at most 16 name cell tiles t with the same t // 32, and in every strip some value of t // 32 is named by exactly 16 slots.
All inputs are finite; a program needn't handle non-finite values.
Results may differ from the reference program's by a relative error of at most 0.0066.
Values may be sent and summed in bfloat16 or wider, within the bound.
A program may use at most 64 MiB of HBM per device.

```python
import jax
import jax.numpy as jnp
from jax import lax

TILE = 256
MAXT = 64
RT_DEV = 8
CT_DEV = 32
ITERS = 2
STRIPS = 8
ROWS = 8192
NCELL = 65536
N_PATH = 4
N_MP = 2


def draw_tile_counts(key, part):
    first, second = jax.random.split(jax.random.fold_in(key, 7))
    base = jax.random.randint(first, (STRIPS,), MAXT // 8, MAXT // 2 + 1)
    order = jax.random.permutation(second, STRIPS)
    return jnp.where(order < max(1, STRIPS // 8), MAXT, base).astype(jnp.int32)


def draw_tile_cols(key, part):
    keys = jax.random.split(jax.random.fold_in(key, 11), 4)
    limit = max(2, max(MAXT // 8, (MAXT + N_PATH - 1) // N_PATH))
    hot_owner = jax.random.randint(keys[0], (STRIPS, 1), 0, N_PATH)
    offset = jax.random.randint(keys[1], (STRIPS, 1), 0, N_PATH - 1)
    slot = jnp.arange(MAXT, dtype=jnp.int32)[None, :]
    others = (hot_owner + 1 + (slot - limit + offset) % (N_PATH - 1)) % N_PATH
    owner = jnp.where(slot < limit, hot_owner, others)
    scores = jax.random.randint(keys[2], (STRIPS, MAXT), 0, 1 << 20) * MAXT + slot
    order = jnp.argsort(scores, axis=1, stable=True)
    owner = jnp.take_along_axis(owner, order, axis=1)
    inside = jax.random.randint(keys[3], (STRIPS, MAXT), 0, CT_DEV)
    return (owner * CT_DEV + inside).reshape(-1).astype(jnp.int32)


def plant(values, key, smallest, top_value):
    dims = values.shape
    spot = [jax.random.randint(jax.random.fold_in(key, axis), (), 0, dims[axis]) for axis in range(len(dims))]
    values = values.at[tuple(spot)].set(smallest)
    longest = dims.index(max(dims))
    spot[longest] = (spot[longest] + 1) % dims[longest]
    return values.at[tuple(spot)].set(top_value)


def shard_levels(stream_key, dims, cuts, low, largest):
    factor_of, own = 1.0, jax.random.fold_in(stream_key, 6)
    for dim, shards_of in cuts:
        steps = jnp.exp(jax.random.uniform(jax.random.fold_in(own, dim), (shards_of,), jnp.float32, low / len(cuts), largest / len(cuts)))
        factor_of = factor_of * jnp.repeat(steps, dims[dim] // shards_of).reshape([-1 if axis == dim else 1 for axis in range(len(dims))])
    return factor_of


def scatter_about(stream_key, extent, width, bound, pieces=(), kind=jnp.bfloat16):
    level = shard_levels(stream_key, extent, pieces, -0.22, 0.18) if pieces else 1.0
    result = jax.random.normal(stream_key, extent, jnp.float32) * width * level
    return jnp.minimum(jnp.maximum(result, -bound), bound).astype(kind)


def setup_inputs(seed: int = 0, part: int = 0) -> dict:
    arg_keys = jax.random.split(jax.random.key(seed), 6)
    own_keys = jax.random.split(jax.random.fold_in(arg_keys[5], part), 6)
    return {
        "tiles": scatter_about(arg_keys[0], (STRIPS * MAXT, TILE, TILE), TILE ** -0.5, 0.375, ((0, 8),)),
        "tile_rows": plant(jax.random.randint(arg_keys[1], (STRIPS * MAXT,), 0, RT_DEV), jax.random.fold_in(arg_keys[1], 1), 0, RT_DEV - 1).astype(jnp.int32),
        "tile_cols": draw_tile_cols(jax.random.fold_in(arg_keys[5], 71), part),
        "tile_counts": draw_tile_counts(jax.random.fold_in(arg_keys[5], 71), part),
        "data": scatter_about(own_keys[4], (ROWS,), 1.0, 6.0, ((0, 4),), jnp.float32),
    }


def reference(tiles, tile_rows, tile_cols, tile_counts, data):
    slots = lax.iota(jnp.int32, STRIPS * MAXT)
    strip = slots // MAXT
    path_index = strip // N_MP
    half_index = strip % N_MP
    live = (slots % MAXT < tile_counts[strip]).astype(jnp.float32)
    cell_tile = (tile_cols // CT_DEV * N_MP + half_index) * CT_DEV + tile_cols % CT_DEV
    row_tile = path_index * RT_DEV + tile_rows
    blocks = tiles.reshape(STRIPS, MAXT, TILE, TILE)

    def forward(vec_b):
        picked = vec_b.reshape(-1, TILE)[cell_tile].reshape(STRIPS, MAXT, TILE)
        prods = lax.map(lambda pair: jnp.einsum('sij,sj->si', pair[0].astype(jnp.float32), pair[1].astype(jnp.float32), precision=lax.Precision.HIGHEST), (blocks, picked))
        prods = prods.reshape(-1, TILE) * live[:, None]
        return jax.ops.segment_sum(prods, row_tile, num_segments=ROWS // TILE).reshape(-1)

    def backward(vec_b):
        picked = vec_b.reshape(-1, TILE)[row_tile].reshape(STRIPS, MAXT, TILE)
        prods = lax.map(lambda pair: jnp.einsum('sij,si->sj', pair[0].astype(jnp.float32), pair[1].astype(jnp.float32), precision=lax.Precision.HIGHEST), (blocks, picked))
        prods = prods.reshape(-1, TILE) * live[:, None]
        return jax.ops.segment_sum(prods, cell_tile, num_segments=NCELL // TILE).reshape(-1)
    beta = jnp.sqrt(jnp.sum(data * data) + 1e-12)
    left = data / beta
    phibar = beta
    right = backward(left.astype(jnp.bfloat16))
    alpha = jnp.sqrt(jnp.sum(right * right) + 1e-12)
    right = right / alpha
    search = right
    rhobar = alpha
    solution = jnp.zeros((NCELL,), jnp.float32)
    for step in range(ITERS):
        left = forward(right.astype(jnp.bfloat16)) - alpha * left
        beta = jnp.sqrt(jnp.sum(left * left) + 1e-12)
        left = left / beta
        right = backward(left.astype(jnp.bfloat16)) - beta * right
        alpha = jnp.sqrt(jnp.sum(right * right) + 1e-12)
        right = right / alpha
        rho = jnp.sqrt(rhobar * rhobar + beta * beta)
        cosine = rhobar / rho
        sine = beta / rho
        theta = sine * alpha
        rhobar = -cosine * alpha
        phi = cosine * phibar
        phibar = sine * phibar
        solution = solution + phi / rho * search
        search = right - theta / rho * search
    return (solution, left * jnp.sqrt(jnp.float32(ROWS)))
```

```python
import functools

import jax
import jax.numpy as jnp
from jax import lax
from jax.experimental import pallas as pl
from jax.experimental.pallas import tpu as pltpu
from jax.sharding import PartitionSpec as P

CT_DEV = 32
CHUNK = 16
GROUP = 8
F32 = jnp.float32
BF16 = jnp.bfloat16


def iota(shape, dim):
    return lax.broadcasted_iota(jnp.int32, shape, dim)


def total(x):
    return jnp.sum(jnp.sum(x, axis=0, keepdims=True), axis=1, keepdims=True)


def split(x):
    hi = x.astype(BF16).astype(F32)
    return hi, x - hi


def kernel(
    npath,
    tiles_hbm,
    rows_ref,
    cols_ref,
    counts_ref,
    data_ref,
    sol_ref,
    left_ref,
    state_ref,
    scal_ref,
    tiles,
    info,
    terms,
    halves_out,
    halves_in,
    sums,
    picks,
    spread,
    lhs,
    prior,
    tile_sem,
    info_sem,
    term_sem,
    half_sem,
    sum_sem,
):
    slots, tile = tiles.shape[0], tiles.shape[1]
    groups, chunks = slots // GROUP, slots // CHUNK
    width = npath * slots
    cells = npath * CT_DEV
    expanded = slots * GROUP
    me = lax.axis_index("path")
    mp = lax.axis_index("mp")

    def tile_copy(g):
        part = pl.ds(g * GROUP, GROUP)
        return pltpu.make_async_copy(tiles_hbm.at[part], tiles.at[part], tile_sem.at[g])

    def peer(step):
        return lax.rem(me + step, npath)

    def sender(step):
        return lax.rem(me + npath - step, npath)

    def to_peer(src, dst, sems, index, step):
        return pltpu.make_async_remote_copy(
            src_ref=src,
            dst_ref=dst,
            send_sem=sems.at[(0, *index)],
            recv_sem=sems.at[(1, *index)],
            device_id={"path": peer(step)},
            device_id_type=pl.DeviceIdType.MESH,
        )

    for g in range(groups):
        tile_copy(g).start()

    barrier = pltpu.get_barrier_semaphore()
    for step in range(1, npath):
        pl.semaphore_signal(
            barrier, inc=1, device_id={"path": peer(step)}, device_id_type=pl.DeviceIdType.MESH
        )
    pl.semaphore_signal(
        barrier, inc=1, device_id={"mp": 1 - mp}, device_id_type=pl.DeviceIdType.MESH
    )

    half_rows = data_ref.shape[0] // 2
    data = jnp.concatenate(
        [data_ref[pl.ds(0, half_rows, stride=2), :], data_ref[pl.ds(1, half_rows, stride=2), :]],
        axis=1,
    )
    live = iota((1, slots), 1) < counts_ref[0]
    row_code = jnp.where(live, rows_ref[...], -1).astype(F32)
    col_live = jnp.where(live, cols_ref[...], -1).astype(F32)

    diag = iota((slots, slots), 0) == iota((slots, slots), 1)
    col_down = jnp.sum(jnp.where(diag, col_live, 0.0), axis=1, keepdims=True)
    here = iota((slots, width), 1) - me * slots == iota((slots, width), 0)
    placed = jnp.sum(jnp.where(here, col_down, 0.0), axis=0, keepdims=True)
    line = iota((8, width), 0)
    info[me] = jnp.where(line == 0, placed, jnp.where(line == 1, total(data * data), 0.0))

    pl.semaphore_wait(barrier, npath)

    def info_copy(step):
        return to_peer(info.at[me], info.at[me], info_sem, (step,), step)

    for step in range(1, npath):
        info_copy(step).start()

    q = iota((2 * slots, slots), 0)
    slot_of_q = q // 16 * 8 + q % 8
    row_q = jnp.sum(
        jnp.where(slot_of_q == iota((2 * slots, slots), 1), row_code, 0.0), axis=1, keepdims=True
    )
    qc = iota((2 * slots, 16), 0)
    offset = (qc % 16 // 8 * 8).astype(F32)
    pick_rows = ((row_q + offset == iota((2 * slots, 16), 1).astype(F32)) & (row_q >= 0)).astype(BF16)

    def term_copy(which, chunk, step):
        part = pl.ds(chunk * CHUNK, CHUNK)
        ref = terms.at[which, me, part]
        return to_peer(ref, ref, term_sem, (which, chunk, step), step)

    def norm_copy(step):
        ref = terms.at[1, me, pl.ds(slots, 16)]
        return to_peer(ref, ref, term_sem, (1, chunks, step), step)

    def backward(which, left):
        hi, lo = split(left)
        both = jnp.concatenate([hi, lo], axis=0).astype(BF16)
        picks[...] = jnp.dot(pick_rows, both, preferred_element_type=F32).astype(BF16)

        def one_chunk(chunk, carry):
            parts = []
            for half in range(CHUNK // GROUP):
                g = chunk * (CHUNK // GROUP) + half
                if which == 0:
                    tile_copy(g).wait()
                block = picks[pl.ds(pl.multiple_of(g * 16, 16), 16), :].astype(F32)
                spot = iota((16, tile), 0) % 8
                acc = jnp.zeros((16, tile), F32)
                for k in range(GROUP):
                    row = jnp.where(spot == k, block, 0.0).astype(BF16)
                    acc = acc + jnp.dot(row, tiles[g * GROUP + k], preferred_element_type=F32)
                parts.append(acc[:8] + acc[8:])
            start = pl.multiple_of(chunk * CHUNK, CHUNK)
            terms[which, me, pl.ds(start, CHUNK), :] = jnp.concatenate(parts, axis=0).astype(BF16)
            for step in range(1, npath):
                term_copy(which, chunk, step).start()
            return carry

        lax.fori_loop(0, chunks, one_chunk, 0)

    def wait_terms(which):
        for chunk in range(chunks):
            for step in range(1, npath):
                term_copy(which, chunk, step).wait()

    def gathered(which):
        block = terms[which, :, :slots, :].reshape(width, tile)
        return jnp.dot(spread[...], block, preferred_element_type=F32)

    def forward(which, right):
        hi, lo = split(right[:expanded].reshape(slots, GROUP, tile))
        lhs[...] = jnp.concatenate([hi, lo], axis=1).astype(BF16)

        def one_group(g, acc):
            for k in range(GROUP):
                s = g * GROUP + k
                acc = acc + lax.dot_general(
                    lhs[s], tiles[s], (((1,), (1,)), ((), ())), preferred_element_type=F32
                )
            return acc

        acc = lax.fori_loop(0, groups, one_group, jnp.zeros((16, tile), F32))
        rest = right[expanded:]
        mine = acc[:8] + acc[8:]
        norm = jnp.broadcast_to(total(rest * rest), (8, 128))
        halves_out[which] = jnp.concatenate([mine, norm], axis=1)
        copy = pltpu.make_async_remote_copy(
            src_ref=halves_out.at[which],
            dst_ref=halves_in.at[which],
            send_sem=half_sem.at[0, which],
            recv_sem=half_sem.at[1, which],
            device_id={"mp": 1 - mp},
            device_id_type=pl.DeviceIdType.MESH,
        )
        copy.start()
        copy.wait()
        both = halves_out[which] + halves_in[which]
        return both[:, :tile], jnp.sqrt(both[:1, tile : tile + 1] + 1e-12)

    backward(0, data)

    for step in range(1, npath):
        info_copy(step).wait()
    facts = info[0]
    for p in range(1, npath):
        facts = facts + info[p]
    all_cols = facts[:1]
    beta0 = jnp.sqrt(facts[1:2, :1] + 1e-12)

    e = iota((expanded, slots), 0)
    mine = iota((expanded, slots), 1) == e // GROUP
    wanted = jnp.where(
        row_code == (e % GROUP).astype(F32), jnp.maximum(cols_ref[...].astype(F32), 0.0), -2.0
    )
    wanted = jnp.sum(jnp.where(mine, wanted, 0.0), axis=1, keepdims=True)
    spread[:expanded] = (wanted == all_cols).astype(BF16)
    spread[expanded:] = (iota((cells, width), 0).astype(F32) == all_cols).astype(BF16)

    wait_terms(0)
    right = gathered(0) / beta0
    prior[...] = right
    product, alpha0 = forward(0, right)
    left0 = data / beta0
    left = product / alpha0 - alpha0 * left0
    n0, n1 = split(total(left * left))
    n1, n2 = split(n1)
    line = iota((16, tile), 0)
    terms[1, me, slots:, :] = jnp.where(
        line == 0, n0, jnp.where(line == 1, n1, jnp.where(line == 2, n2, 0.0))
    ).astype(BF16)
    for step in range(1, npath):
        norm_copy(step).start()
    backward(1, left)
    for step in range(1, npath):
        norm_copy(step).wait()
    norms = jnp.sum(terms[1, :, slots:, :128].astype(F32).reshape(npath * 16, 128), axis=0, keepdims=True)
    beta1 = jnp.sqrt(norms[:, :1] + 1e-12)
    left = left / beta1
    wait_terms(1)
    right = gathered(1) / beta1 - (beta1 / alpha0) * prior[...]
    own = pl.ds(expanded + me * CT_DEV, CT_DEV)
    search = prior[own, :] / alpha0
    prior[...] = right
    product, alpha1 = forward(1, right)
    left = product / alpha1 - alpha1 * left
    sums[me] = jnp.broadcast_to(total(left * left), (8, 128))

    def sum_copy(step):
        return to_peer(sums.at[me], sums.at[me], sum_sem, (step,), step)

    for step in range(1, npath):
        sum_copy(step).start()

    state = prior[own, :] / alpha1
    rho = jnp.sqrt(alpha0 * alpha0 + beta1 * beta1)
    cosine, sine = alpha0 / rho, beta1 / rho
    theta = sine * alpha1
    rhobar = -cosine * alpha1
    phi = cosine * beta0
    phibar = sine * beta0
    first = phi / rho * search
    search = state - theta / rho * search
    state_ref[...] = state

    for step in range(1, npath):
        sum_copy(step).wait()
    norm = sums[0]
    for p in range(1, npath):
        norm = norm + sums[p]
    beta2 = jnp.sqrt(norm[:1, :1] + 1e-12)
    left = left / beta2 * jnp.sqrt(F32(npath * half_rows * tile))
    rho = jnp.sqrt(rhobar * rhobar + beta2 * beta2)
    phi = rhobar / rho * phibar
    answer = first + phi / rho * search
    for h in range(2):
        cut = slice(h * 128, h * 128 + 128)
        sol_ref[pl.ds(h, CT_DEV, stride=2), :] = answer[:, cut]
        left_ref[pl.ds(h, half_rows, stride=2), :] = left[:, cut]
    scal_ref[...] = jnp.broadcast_to(beta2, scal_ref.shape)


def last_right_step(tiles, tile_rows, tile_cols, tile_counts, left, beta, state):
    slots, tile = tiles.shape[0], tiles.shape[1]
    npath = lax.axis_size("path")
    live = lax.iota(jnp.int32, slots) < tile_counts[0]
    picked = left.reshape(-1, tile).astype(BF16)[tile_rows]
    prods = jnp.einsum("sij,si->sj", tiles, picked, preferred_element_type=F32)
    place = (lax.iota(jnp.int32, npath * CT_DEV)[:, None] == tile_cols[None, :]) & live[None, :]
    cells = jnp.dot(place.astype(F32), prods, precision=lax.Precision.HIGHEST)
    own = lax.psum_scatter(cells, "path", scatter_dimension=0, tiled=True) - beta * state
    alpha = jnp.sqrt(lax.psum(jnp.sum(own * own), ("path", "mp")) + 1e-12)
    return own / alpha, alpha


def on_device(tiles, tile_rows, tile_cols, tile_counts, data):
    slots, tile = tiles.shape[0], tiles.shape[1]
    npath = lax.axis_size("path")
    row_tiles = data.shape[0] // tile
    width, lines = npath * slots, slots * GROUP + npath * CT_DEV
    chunks = slots // CHUNK
    vmem = pl.BlockSpec(memory_space=pltpu.VMEM)
    answer, left, state, beta = pl.pallas_call(
        functools.partial(kernel, npath),
        out_shape=(
            jax.ShapeDtypeStruct((CT_DEV * tile // 128, 128), F32),
            jax.ShapeDtypeStruct((row_tiles * tile // 128, 128), F32),
            jax.ShapeDtypeStruct((CT_DEV, tile), F32),
            jax.ShapeDtypeStruct((8, 128), F32),
        ),
        in_specs=[
            pl.BlockSpec(memory_space=pl.ANY),
            vmem,
            vmem,
            pl.BlockSpec(memory_space=pltpu.SMEM),
            vmem,
        ],
        out_specs=(vmem,) * 4,
        scratch_shapes=[
            pltpu.VMEM((slots, tile, tile), BF16),
            pltpu.VMEM((npath, 8, width), F32),
            pltpu.VMEM((2, npath, slots + 16, tile), BF16),
            pltpu.VMEM((2, 8, tile + 128), F32),
            pltpu.VMEM((2, 8, tile + 128), F32),
            pltpu.VMEM((npath, 8, 128), F32),
            pltpu.VMEM((2 * slots, tile), BF16),
            pltpu.VMEM((lines, width), BF16),
            pltpu.VMEM((slots, 16, tile), BF16),
            pltpu.VMEM((lines, tile), F32),
            pltpu.SemaphoreType.DMA((slots // GROUP,)),
            pltpu.SemaphoreType.DMA((2, npath)),
            pltpu.SemaphoreType.DMA((2, 2, chunks + 1, npath)),
            pltpu.SemaphoreType.DMA((2, 2)),
            pltpu.SemaphoreType.DMA((2, npath)),
        ],
        compiler_params=pltpu.CompilerParams(
            collective_id=0, has_side_effects=True, vmem_limit_bytes=48 * 1024 * 1024
        ),
        cost_estimate=pl.CostEstimate(
            flops=8 * 16 * slots * tile * tile,
            bytes_accessed=2 * slots * tile * tile,
            transcendentals=0,
        ),
    )(
        tiles,
        tile_rows.reshape(1, slots),
        tile_cols.reshape(1, slots),
        tile_counts,
        data.reshape(-1, 128),
    )
    left = left.reshape(-1)
    last_right_step(
        tiles,
        tile_rows,
        tile_cols,
        tile_counts,
        left / jnp.sqrt(F32(row_tiles * tile * npath)),
        beta[0, 0],
        state,
    )
    return answer.reshape(-1), left


def solution(mesh):
    placed = (
        P(("path", "mp"), None, None),
        P(("path", "mp")),
        P(("path", "mp")),
        P(("path", "mp")),
        P(("period", "path")),
    )
    return jax.shard_map(
        on_device,
        mesh=mesh,
        in_specs=placed,
        out_specs=(P(("period", "path", "mp")), P(("period", "path"))),
        check_vma=False,
    )
```

```python
import functools

import jax
import jax.numpy as jnp
from jax import lax
from jax.experimental import pallas as pl
from jax.experimental.pallas import tpu as pltpu
from jax.sharding import PartitionSpec as P

CT_DEV = 32
CHUNK = 16
GROUP = 8
F32 = jnp.float32
BF16 = jnp.bfloat16


def iota(shape, dim):
    return lax.broadcasted_iota(jnp.int32, shape, dim)


def total(x):
    return jnp.sum(jnp.sum(x, axis=0, keepdims=True), axis=1, keepdims=True)


def split(x):
    hi = x.astype(BF16).astype(F32)
    return hi, x - hi


def kernel(
    npath,
    tiles_hbm,
    rows_hbm,
    cols_hbm,
    counts_hbm,
    data_hbm,
    pack_hbm,
    rows_ref,
    cols_ref,
    counts_ref,
    data_ref,
    pack_ref,
    tiles,
    info,
    terms,
    halves_out,
    halves_in,
    sums,
    picks,
    spread,
    lhs,
    prior,
    small_sem,
    out_sem,
    tile_sem,
    info_sem,
    term_sem,
    half_sem,
    sum_sem,
):
    slots, tile = tiles.shape[0], tiles.shape[1]
    groups, chunks = slots // GROUP, slots // CHUNK
    width = npath * slots
    cells = npath * CT_DEV
    expanded = slots * GROUP
    me = lax.axis_index("path")
    mp = lax.axis_index("mp")

    def tile_copy(g):
        part = pl.ds(g * GROUP, GROUP)
        return pltpu.make_async_copy(tiles_hbm.at[part], tiles.at[part], tile_sem.at[g])

    def peer(step):
        return lax.rem(me + step, npath)

    def sender(step):
        return lax.rem(me + npath - step, npath)

    def to_peer(src, dst, sems, index, step):
        return pltpu.make_async_remote_copy(
            src_ref=src,
            dst_ref=dst,
            send_sem=sems.at[(0, *index)],
            recv_sem=sems.at[(1, *index)],
            device_id={"path": peer(step)},
            device_id_type=pl.DeviceIdType.MESH,
        )

    smalls = [
        pltpu.make_async_copy(src, dst, small_sem.at[i])
        for i, (src, dst) in enumerate(
            (
                (data_hbm, data_ref),
                (rows_hbm, rows_ref),
                (cols_hbm, cols_ref),
                (counts_hbm, counts_ref),
            )
        )
    ]
    for copy in smalls:
        copy.start()
    for g in range(groups):
        tile_copy(g).start()

    barrier = pltpu.get_barrier_semaphore()
    for step in range(1, npath):
        pl.semaphore_signal(
            barrier, inc=1, device_id={"path": peer(step)}, device_id_type=pl.DeviceIdType.MESH
        )
    pl.semaphore_signal(
        barrier, inc=1, device_id={"mp": 1 - mp}, device_id_type=pl.DeviceIdType.MESH
    )

    for copy in smalls:
        copy.wait()
    half_rows = data_ref.shape[0] // 2
    data = jnp.concatenate(
        [data_ref[pl.ds(0, half_rows, stride=2), :], data_ref[pl.ds(1, half_rows, stride=2), :]],
        axis=1,
    )
    live = iota((1, slots), 1) < counts_ref[0]
    row_code = jnp.where(live, rows_ref[...], -1).astype(F32)
    col_live = jnp.where(live, cols_ref[...], -1).astype(F32)

    diag = iota((slots, slots), 0) == iota((slots, slots), 1)
    col_down = jnp.sum(jnp.where(diag, col_live, 0.0), axis=1, keepdims=True)
    here = iota((slots, width), 1) - me * slots == iota((slots, width), 0)
    placed = jnp.sum(jnp.where(here, col_down, 0.0), axis=0, keepdims=True)
    line = iota((8, width), 0)
    info[me] = jnp.where(line == 0, placed, jnp.where(line == 1, total(data * data), 0.0))

    pl.semaphore_wait(barrier, npath)

    def info_copy(step):
        return to_peer(info.at[me], info.at[me], info_sem, (step,), step)

    for step in range(1, npath):
        info_copy(step).start()

    q = iota((2 * slots, slots), 0)
    slot_of_q = q // 16 * 8 + q % 8
    row_q = jnp.sum(
        jnp.where(slot_of_q == iota((2 * slots, slots), 1), row_code, 0.0), axis=1, keepdims=True
    )
    qc = iota((2 * slots, 16), 0)
    offset = (qc % 16 // 8 * 8).astype(F32)
    pick_rows = ((row_q + offset == iota((2 * slots, 16), 1).astype(F32)) & (row_q >= 0)).astype(BF16)

    def term_copy(which, chunk, step):
        part = pl.ds(chunk * CHUNK, CHUNK)
        ref = terms.at[which, me, part]
        return to_peer(ref, ref, term_sem, (which, chunk, step), step)

    def norm_copy(step):
        ref = terms.at[1, me, pl.ds(slots, 16)]
        return to_peer(ref, ref, term_sem, (1, chunks, step), step)

    def backward(which, left):
        hi, lo = split(left)
        both = jnp.concatenate([hi, lo], axis=0).astype(BF16)
        picks[...] = jnp.dot(pick_rows, both, preferred_element_type=F32).astype(BF16)

        def one_chunk(chunk, carry):
            parts = []
            for half in range(CHUNK // GROUP):
                g = chunk * (CHUNK // GROUP) + half
                if which == 0:
                    tile_copy(g).wait()
                block = picks[pl.ds(pl.multiple_of(g * 16, 16), 16), :].astype(F32)
                spot = iota((16, tile), 0) % 8
                acc = jnp.zeros((16, tile), F32)
                for k in range(GROUP):
                    row = jnp.where(spot == k, block, 0.0).astype(BF16)
                    acc = acc + jnp.dot(row, tiles[g * GROUP + k], preferred_element_type=F32)
                parts.append(acc[:8] + acc[8:])
            start = pl.multiple_of(chunk * CHUNK, CHUNK)
            terms[which, me, pl.ds(start, CHUNK), :] = jnp.concatenate(parts, axis=0).astype(BF16)
            for step in range(1, npath):
                term_copy(which, chunk, step).start()
            return carry

        lax.fori_loop(0, chunks, one_chunk, 0)

    def wait_terms(which):
        for chunk in range(chunks):
            for step in range(1, npath):
                term_copy(which, chunk, step).wait()

    def gathered(which):
        block = terms[which, :, :slots, :].reshape(width, tile)
        return jnp.dot(spread[...], block, preferred_element_type=F32)

    def forward(which, right):
        hi, lo = split(right[:expanded].reshape(slots, GROUP, tile))
        lhs[...] = jnp.concatenate([hi, lo], axis=1).astype(BF16)

        def one_group(g, acc):
            for k in range(GROUP):
                s = g * GROUP + k
                acc = acc + lax.dot_general(
                    lhs[s], tiles[s], (((1,), (1,)), ((), ())), preferred_element_type=F32
                )
            return acc

        acc = lax.fori_loop(0, groups, one_group, jnp.zeros((16, tile), F32))
        rest = right[expanded:]
        mine = acc[:8] + acc[8:]
        norm = jnp.broadcast_to(total(rest * rest), (8, 128))
        halves_out[which] = jnp.concatenate([mine, norm], axis=1)
        copy = pltpu.make_async_remote_copy(
            src_ref=halves_out.at[which],
            dst_ref=halves_in.at[which],
            send_sem=half_sem.at[0, which],
            recv_sem=half_sem.at[1, which],
            device_id={"mp": 1 - mp},
            device_id_type=pl.DeviceIdType.MESH,
        )
        copy.start()
        copy.wait()
        both = halves_out[which] + halves_in[which]
        return both[:, :tile], jnp.sqrt(both[:1, tile : tile + 1] + 1e-12)

    backward(0, data)

    for step in range(1, npath):
        info_copy(step).wait()
    facts = info[0]
    for p in range(1, npath):
        facts = facts + info[p]
    all_cols = facts[:1]
    beta0 = jnp.sqrt(facts[1:2, :1] + 1e-12)

    e = iota((expanded, slots), 0)
    mine = iota((expanded, slots), 1) == e // GROUP
    wanted = jnp.where(
        row_code == (e % GROUP).astype(F32), jnp.maximum(cols_ref[...].astype(F32), 0.0), -2.0
    )
    wanted = jnp.sum(jnp.where(mine, wanted, 0.0), axis=1, keepdims=True)
    spread[:expanded] = (wanted == all_cols).astype(BF16)
    spread[expanded:] = (iota((cells, width), 0).astype(F32) == all_cols).astype(BF16)

    wait_terms(0)
    right = gathered(0) / beta0
    prior[...] = right
    product, alpha0 = forward(0, right)
    left0 = data / beta0
    left = product / alpha0 - alpha0 * left0
    n0, n1 = split(total(left * left))
    n1, n2 = split(n1)
    line = iota((16, tile), 0)
    terms[1, me, slots:, :] = jnp.where(
        line == 0, n0, jnp.where(line == 1, n1, jnp.where(line == 2, n2, 0.0))
    ).astype(BF16)
    for step in range(1, npath):
        norm_copy(step).start()
    backward(1, left)
    for step in range(1, npath):
        norm_copy(step).wait()
    norms = jnp.sum(terms[1, :, slots:, :128].astype(F32).reshape(npath * 16, 128), axis=0, keepdims=True)
    beta1 = jnp.sqrt(norms[:, :1] + 1e-12)
    left = left / beta1
    wait_terms(1)
    right = gathered(1) / beta1 - (beta1 / alpha0) * prior[...]
    own = pl.ds(expanded + me * CT_DEV, CT_DEV)
    search = prior[own, :] / alpha0
    prior[...] = right
    product, alpha1 = forward(1, right)
    left = product / alpha1 - alpha1 * left
    sums[me] = jnp.broadcast_to(total(left * left), (8, 128))

    def sum_copy(step):
        return to_peer(sums.at[me], sums.at[me], sum_sem, (step,), step)

    for step in range(1, npath):
        sum_copy(step).start()

    state = prior[own, :] / alpha1
    rho = jnp.sqrt(alpha0 * alpha0 + beta1 * beta1)
    cosine, sine = alpha0 / rho, beta1 / rho
    theta = sine * alpha1
    rhobar = -cosine * alpha1
    phi = cosine * beta0
    phibar = sine * beta0
    first = phi / rho * search
    search = state - theta / rho * search

    def keep(block, base):
        lines = block.shape[0]
        for h in range(2):
            pack_ref[pl.ds(base + h, lines, stride=2), :] = block[:, h * 128 : h * 128 + 128]

    def pack_copy(base, lines, i):
        part = pl.ds(base, lines)
        return pltpu.make_async_copy(pack_ref.at[part], pack_hbm.at[part], out_sem.at[i])

    result_lines = pack_ref.shape[0] - 2 * CT_DEV
    keep(state, result_lines)
    state_copy = pack_copy(result_lines, 2 * CT_DEV, 0)
    state_copy.start()

    for step in range(1, npath):
        sum_copy(step).wait()
    norm = sums[0]
    for p in range(1, npath):
        norm = norm + sums[p]
    beta2 = jnp.sqrt(norm[:1, :1] + 1e-12)
    left = left / beta2 * jnp.sqrt(F32(npath * half_rows * tile))
    rho = jnp.sqrt(rhobar * rhobar + beta2 * beta2)
    phi = rhobar / rho * phibar
    answer = first + phi / rho * search
    keep(answer, 0)
    keep(left, 2 * CT_DEV)
    pack_ref[result_lines - 8 : result_lines] = jnp.broadcast_to(beta2, (8, 128))
    result_copy = pack_copy(0, result_lines, 1)
    result_copy.start()
    state_copy.wait()
    result_copy.wait()


def unpack(pack_hbm, answer_hbm, left_hbm, sem):
    base = 0
    copies = []
    for i, ref in enumerate((answer_hbm, left_hbm)):
        part = pack_hbm.at[pl.ds(base, ref.shape[0])]
        copies.append(pltpu.make_async_copy(part, ref, sem.at[i]))
        base += ref.shape[0]
    for copy in copies:
        copy.start()
    for copy in copies:
        copy.wait()


def last_right_step(tiles, tile_rows, tile_cols, tile_counts, left, beta, state):
    slots, tile = tiles.shape[0], tiles.shape[1]
    npath = lax.axis_size("path")
    live = lax.iota(jnp.int32, slots) < tile_counts[0]
    picked = left.reshape(-1, tile).astype(BF16)[tile_rows]
    prods = jnp.einsum("sij,si->sj", tiles, picked, preferred_element_type=F32)
    place = (lax.iota(jnp.int32, npath * CT_DEV)[:, None] == tile_cols[None, :]) & live[None, :]
    cells = jnp.dot(place.astype(F32), prods, precision=lax.Precision.HIGHEST)
    own = lax.psum_scatter(cells, "path", scatter_dimension=0, tiled=True) - beta * state
    alpha = jnp.sqrt(lax.psum(jnp.sum(own * own), ("path", "mp")) + 1e-12)
    return own / alpha, alpha


def on_device(tiles, tile_rows, tile_cols, tile_counts, data):
    slots, tile = tiles.shape[0], tiles.shape[1]
    npath = lax.axis_size("path")
    row_tiles = data.shape[0] // tile
    width, lines = npath * slots, slots * GROUP + npath * CT_DEV
    chunks = slots // CHUNK
    hbm = pl.BlockSpec(memory_space=pltpu.HBM)
    answer_lines, left_lines = CT_DEV * tile // 128, row_tiles * tile // 128
    pack = pl.pallas_call(
        functools.partial(kernel, npath),
        out_shape=jax.ShapeDtypeStruct((2 * answer_lines + left_lines + 8, 128), F32),
        in_specs=[hbm] * 5,
        out_specs=hbm,
        scratch_shapes=[
            pltpu.VMEM((1, slots), jnp.int32),
            pltpu.VMEM((1, slots), jnp.int32),
            pltpu.SMEM((1,), jnp.int32),
            pltpu.VMEM((left_lines, 128), F32),
            pltpu.VMEM((2 * answer_lines + left_lines + 8, 128), F32),
            pltpu.VMEM((slots, tile, tile), BF16),
            pltpu.VMEM((npath, 8, width), F32),
            pltpu.VMEM((2, npath, slots + 16, tile), BF16),
            pltpu.VMEM((2, 8, tile + 128), F32),
            pltpu.VMEM((2, 8, tile + 128), F32),
            pltpu.VMEM((npath, 8, 128), F32),
            pltpu.VMEM((2 * slots, tile), BF16),
            pltpu.VMEM((lines, width), BF16),
            pltpu.VMEM((slots, 16, tile), BF16),
            pltpu.VMEM((lines, tile), F32),
            pltpu.SemaphoreType.DMA((4,)),
            pltpu.SemaphoreType.DMA((2,)),
            pltpu.SemaphoreType.DMA((slots // GROUP,)),
            pltpu.SemaphoreType.DMA((2, npath)),
            pltpu.SemaphoreType.DMA((2, 2, chunks + 1, npath)),
            pltpu.SemaphoreType.DMA((2, 2)),
            pltpu.SemaphoreType.DMA((2, npath)),
        ],
        compiler_params=pltpu.CompilerParams(
            collective_id=0, has_side_effects=True, vmem_limit_bytes=64 * 1024 * 1024 - 65536
        ),
        cost_estimate=pl.CostEstimate(
            flops=8 * 16 * slots * tile * tile,
            bytes_accessed=2 * slots * tile * tile,
            transcendentals=0,
        ),
    )(
        tiles,
        tile_rows.reshape(1, slots),
        tile_cols.reshape(1, slots),
        tile_counts,
        data.reshape(-1, 128),
    )
    answer, left = pl.pallas_call(
        unpack,
        out_shape=(
            jax.ShapeDtypeStruct((answer_lines, 128), F32),
            jax.ShapeDtypeStruct((left_lines, 128), F32),
        ),
        in_specs=[hbm],
        out_specs=(hbm, hbm),
        scratch_shapes=[pltpu.SemaphoreType.DMA((2,))],
    )(pack)
    left = left.reshape(-1)
    state = pack[answer_lines + left_lines + 8 :].reshape(CT_DEV, tile)
    last_right_step(
        tiles,
        tile_rows,
        tile_cols,
        tile_counts,
        left / jnp.sqrt(F32(row_tiles * tile * npath)),
        pack[answer_lines + left_lines, 0],
        state,
    )
    return answer.reshape(-1), left


def solution(mesh):
    placed = (
        P(("path", "mp"), None, None),
        P(("path", "mp")),
        P(("path", "mp")),
        P(("path", "mp")),
        P(("period", "path")),
    )
    return jax.shard_map(
        on_device,
        mesh=mesh,
        in_specs=placed,
        out_specs=(P(("period", "path", "mp")), P(("period", "path"))),
        check_vma=False,
    )
```

```python
import functools

import jax
import jax.numpy as jnp
from jax import lax
from jax.experimental import pallas as pl
from jax.experimental.pallas import tpu as pltpu
from jax.sharding import PartitionSpec as P

CT_DEV = 32
CHUNK = 16
GROUP = 8
VMEM_LIMIT = 56 * 1024 * 1024
F32 = jnp.float32
BF16 = jnp.bfloat16


def iota(shape, dim):
    return lax.broadcasted_iota(jnp.int32, shape, dim)


def total(x):
    return jnp.sum(jnp.sum(x, axis=0, keepdims=True), axis=1, keepdims=True)


def split(x):
    hi = x.astype(BF16).astype(F32)
    return hi, x - hi


def kernel(
    npath,
    tiles_hbm,
    rows_hbm,
    cols_hbm,
    counts_hbm,
    data_hbm,
    pack_ref,
    rows_ref,
    cols_ref,
    counts_ref,
    data_ref,
    tiles,
    info,
    terms,
    halves_out,
    halves_in,
    sums,
    picks,
    spread,
    prods,
    prior,
    small_sem,
    tile_sem,
    info_sem,
    term_sem,
    half_sem,
    sum_sem,
):
    slots, tile = tiles.shape[0], tiles.shape[1]
    groups, chunks = slots // GROUP, slots // CHUNK
    width = npath * slots
    cells = npath * CT_DEV
    me = lax.axis_index("path")
    mp = lax.axis_index("mp")

    def tile_copy(g):
        part = pl.ds(g * GROUP, GROUP)
        return pltpu.make_async_copy(tiles_hbm.at[part], tiles.at[part], tile_sem.at[g])

    def peer(step):
        return lax.rem(me + step, npath)

    def sender(step):
        return lax.rem(me + npath - step, npath)

    def to_peer(src, dst, sems, index, step):
        return pltpu.make_async_remote_copy(
            src_ref=src,
            dst_ref=dst,
            send_sem=sems.at[(0, *index)],
            recv_sem=sems.at[(1, *index)],
            device_id={"path": peer(step)},
            device_id_type=pl.DeviceIdType.MESH,
        )

    smalls = [
        pltpu.make_async_copy(src, dst, small_sem.at[i])
        for i, (src, dst) in enumerate(
            (
                (data_hbm, data_ref),
                (rows_hbm, rows_ref),
                (cols_hbm, cols_ref),
                (counts_hbm, counts_ref),
            )
        )
    ]
    for copy in smalls:
        copy.start()
    for g in range(groups):
        tile_copy(g).start()

    barrier = pltpu.get_barrier_semaphore()
    for step in range(1, npath):
        pl.semaphore_signal(
            barrier, inc=1, device_id={"path": peer(step)}, device_id_type=pl.DeviceIdType.MESH
        )
    pl.semaphore_signal(
        barrier, inc=1, device_id={"mp": 1 - mp}, device_id_type=pl.DeviceIdType.MESH
    )

    for copy in smalls:
        copy.wait()
    half_rows = data_ref.shape[0] // 2
    data = jnp.concatenate(
        [data_ref[pl.ds(0, half_rows, stride=2), :], data_ref[pl.ds(1, half_rows, stride=2), :]],
        axis=1,
    )
    live = iota((1, slots), 1) < counts_ref[0]
    row_code = jnp.where(live, rows_ref[...], -1).astype(F32)
    col_live = jnp.where(live, cols_ref[...], -1).astype(F32)

    diag = iota((slots, slots), 0) == iota((slots, slots), 1)
    col_down = jnp.sum(jnp.where(diag, col_live, 0.0), axis=1, keepdims=True)
    here = iota((slots, width), 1) - me * slots == iota((slots, width), 0)
    placed = jnp.sum(jnp.where(here, col_down, 0.0), axis=0, keepdims=True)
    line = iota((8, width), 0)
    info[me] = jnp.where(line == 0, placed, jnp.where(line == 1, total(data * data), 0.0))

    pl.semaphore_wait(barrier, npath)

    def info_copy(step):
        return to_peer(info.at[me], info.at[me], info_sem, (step,), step)

    for step in range(1, npath):
        info_copy(step).start()

    q = iota((2 * slots, slots), 0)
    slot_of_q = q // 16 * 8 + q % 8
    row_q = jnp.sum(
        jnp.where(slot_of_q == iota((2 * slots, slots), 1), row_code, 0.0), axis=1, keepdims=True
    )
    qc = iota((2 * slots, 16), 0)
    offset = (qc % 16 // 8 * 8).astype(F32)
    pick_rows = ((row_q + offset == iota((2 * slots, 16), 1).astype(F32)) & (row_q >= 0)).astype(BF16)

    row_down = jnp.sum(jnp.where(diag, row_code, 0.0), axis=1, keepdims=True)
    q = iota((slots, 2 * slots), 1)
    slot_of_q = q // 16 * 8 + q % 8
    row_q = jnp.sum(
        jnp.where(slot_of_q == iota((slots, 2 * slots), 0), row_down, 0.0), axis=0, keepdims=True
    )
    offset = (iota((16, 2 * slots), 1) % 16 // 8 * 8).astype(F32)
    sum_rows = (
        (row_q + offset == iota((16, 2 * slots), 0).astype(F32)) & (row_q >= 0)
    ).astype(BF16)

    def term_copy(which, chunk, step):
        part = pl.ds(chunk * CHUNK, CHUNK)
        ref = terms.at[which, me, part]
        return to_peer(ref, ref, term_sem, (which, chunk, step), step)

    def norm_copy(step):
        ref = terms.at[1, me, pl.ds(slots, 16)]
        return to_peer(ref, ref, term_sem, (1, chunks, step), step)

    def fan_out(block):
        spot = iota((16, tile), 0) % 8
        rows = [jnp.where(spot == k, block, 0.0).astype(BF16) for k in range(GROUP)]
        return jnp.concatenate(rows, axis=1)

    def backward(which, left):
        hi, lo = split(left)
        both = jnp.concatenate([hi, lo], axis=0).astype(BF16)
        picks[...] = jnp.dot(pick_rows, both, preferred_element_type=F32).astype(BF16)

        def one_chunk(chunk, carry):
            parts = []
            for half in range(CHUNK // GROUP):
                g = chunk * (CHUNK // GROUP) + half
                if which == 0:
                    tile_copy(g).wait()
                block = picks[pl.ds(pl.multiple_of(g * 16, 16), 16), :].astype(F32)
                acc = jnp.dot(
                    fan_out(block),
                    tiles[pl.ds(g * GROUP, GROUP)].reshape(GROUP * tile, tile),
                    preferred_element_type=F32,
                )
                parts.append(acc[:8] + acc[8:])
            start = pl.multiple_of(chunk * CHUNK, CHUNK)
            terms[which, me, pl.ds(start, CHUNK), :] = jnp.concatenate(parts, axis=0).astype(BF16)
            for step in range(1, npath):
                term_copy(which, chunk, step).start()
            return carry

        lax.fori_loop(0, chunks, one_chunk, 0)

    def wait_terms(which):
        for chunk in range(chunks):
            for step in range(1, npath):
                term_copy(which, chunk, step).wait()

    def gathered(which):
        block = terms[which, :, :slots, :].reshape(width, tile)
        return jnp.dot(spread[...], block, preferred_element_type=F32)

    def forward(which, right):
        hi, lo = split(right[:slots].reshape(groups, GROUP, tile))
        both = jnp.concatenate([hi, lo], axis=1)
        picks[...] = both.reshape(2 * slots, tile).astype(BF16)

        def two_groups(pair, carry):
            for half in range(2):
                g = pair * 2 + half
                block = picks[pl.ds(pl.multiple_of(g * 16, 16), 16), :].astype(F32)
                wide = fan_out(block)
                acc = jnp.zeros((16, tile), F32)
                for k in range(GROUP):
                    acc = acc + lax.dot_general(
                        wide[:, k * tile : k * tile + tile],
                        tiles[g * GROUP + k],
                        (((1,), (1,)), ((), ())),
                        preferred_element_type=F32,
                    )
                prods[g] = acc[:8] + acc[8:]
            return carry

        lax.fori_loop(0, groups // 2, two_groups, 0)
        hi, lo = split(prods[...])
        both = jnp.concatenate([hi, lo], axis=1).reshape(2 * slots, tile).astype(BF16)
        acc = jnp.dot(sum_rows, both, preferred_element_type=F32)
        rest = right[slots:]
        mine = acc[:8] + acc[8:]
        norm = jnp.broadcast_to(total(rest * rest), (8, 128))
        halves_out[which] = jnp.concatenate([mine, norm], axis=1)
        copy = pltpu.make_async_remote_copy(
            src_ref=halves_out.at[which],
            dst_ref=halves_in.at[which],
            send_sem=half_sem.at[0, which],
            recv_sem=half_sem.at[1, which],
            device_id={"mp": 1 - mp},
            device_id_type=pl.DeviceIdType.MESH,
        )
        copy.start()
        copy.wait()
        both = halves_out[which] + halves_in[which]
        return both[:, :tile], jnp.sqrt(both[:1, tile : tile + 1] + 1e-12)

    backward(0, data)

    for step in range(1, npath):
        info_copy(step).wait()
    facts = info[0]
    for p in range(1, npath):
        facts = facts + info[p]
    all_cols = facts[:1]
    beta0 = jnp.sqrt(facts[1:2, :1] + 1e-12)

    col_all_down = jnp.sum(
        jnp.where(diag, cols_ref[...].astype(F32), 0.0), axis=1, keepdims=True
    )
    spread[:slots] = (col_all_down == all_cols).astype(BF16)
    spread[slots:] = (iota((cells, width), 0).astype(F32) == all_cols).astype(BF16)

    wait_terms(0)
    right = gathered(0) / beta0
    prior[...] = right
    product, alpha0 = forward(0, right)
    left0 = data / beta0
    left = product / alpha0 - alpha0 * left0
    n0, n1 = split(total(left * left))
    n1, n2 = split(n1)
    line = iota((16, tile), 0)
    terms[1, me, slots:, :] = jnp.where(
        line == 0, n0, jnp.where(line == 1, n1, jnp.where(line == 2, n2, 0.0))
    ).astype(BF16)
    for step in range(1, npath):
        norm_copy(step).start()
    backward(1, left)
    for step in range(1, npath):
        norm_copy(step).wait()
    norms = jnp.sum(terms[1, :, slots:, :128].astype(F32).reshape(npath * 16, 128), axis=0, keepdims=True)
    beta1 = jnp.sqrt(norms[:, :1] + 1e-12)
    left = left / beta1
    wait_terms(1)
    right = gathered(1) / beta1 - (beta1 / alpha0) * prior[...]
    own = pl.ds(slots + me * CT_DEV, CT_DEV)
    search = prior[own, :] / alpha0
    prior[...] = right
    product, alpha1 = forward(1, right)
    left = product / alpha1 - alpha1 * left
    sums[me] = jnp.broadcast_to(total(left * left), (8, 128))

    def sum_copy(step):
        return to_peer(sums.at[me], sums.at[me], sum_sem, (step,), step)

    for step in range(1, npath):
        sum_copy(step).start()

    state = prior[own, :] / alpha1
    rho = jnp.sqrt(alpha0 * alpha0 + beta1 * beta1)
    cosine, sine = alpha0 / rho, beta1 / rho
    theta = sine * alpha1
    rhobar = -cosine * alpha1
    phi = cosine * beta0
    phibar = sine * beta0
    first = phi / rho * search
    search = state - theta / rho * search

    def keep(block, base):
        lines = block.shape[0]
        for h in range(2):
            pack_ref[pl.ds(base + h, lines, stride=2), :] = block[:, h * 128 : h * 128 + 128]

    result_lines = pack_ref.shape[0] - 2 * CT_DEV
    keep(state, result_lines)

    for step in range(1, npath):
        sum_copy(step).wait()
    norm = sums[0]
    for p in range(1, npath):
        norm = norm + sums[p]
    beta2 = jnp.sqrt(norm[:1, :1] + 1e-12)
    left = left / beta2 * jnp.sqrt(F32(npath * half_rows * tile))
    rho = jnp.sqrt(rhobar * rhobar + beta2 * beta2)
    phi = rhobar / rho * phibar
    answer = first + phi / rho * search
    keep(answer, 0)
    keep(left, 2 * CT_DEV)
    pack_ref[result_lines - 8 : result_lines] = jnp.broadcast_to(beta2, (8, 128))


def unpack(pack_ref, answer_hbm, left_hbm, sem):
    base = 0
    copies = []
    for i, ref in enumerate((answer_hbm, left_hbm)):
        part = pack_ref.at[pl.ds(base, ref.shape[0])]
        copies.append(pltpu.make_async_copy(part, ref, sem.at[i]))
        base += ref.shape[0]
    for copy in copies:
        copy.start()
    for copy in copies:
        copy.wait()


def last_right_step(tiles, tile_rows, tile_cols, tile_counts, left, beta, state):
    slots, tile = tiles.shape[0], tiles.shape[1]
    npath = lax.axis_size("path")
    live = lax.iota(jnp.int32, slots) < tile_counts[0]
    picked = left.reshape(-1, tile).astype(BF16)[tile_rows]
    prods = jnp.einsum("sij,si->sj", tiles, picked, preferred_element_type=F32)
    place = (lax.iota(jnp.int32, npath * CT_DEV)[:, None] == tile_cols[None, :]) & live[None, :]
    cells = jnp.dot(place.astype(F32), prods, precision=lax.Precision.HIGHEST)
    own = lax.psum_scatter(cells, "path", scatter_dimension=0, tiled=True) - beta * state
    alpha = jnp.sqrt(lax.psum(jnp.sum(own * own), ("path", "mp")) + 1e-12)
    return own / alpha, alpha


def on_device(tiles, tile_rows, tile_cols, tile_counts, data):
    slots, tile = tiles.shape[0], tiles.shape[1]
    npath = lax.axis_size("path")
    row_tiles = data.shape[0] // tile
    width, lines = npath * slots, slots + npath * CT_DEV
    chunks = slots // CHUNK
    hbm = pl.BlockSpec(memory_space=pltpu.HBM)
    vmem = pl.BlockSpec(memory_space=pltpu.VMEM)
    answer_lines, left_lines = CT_DEV * tile // 128, row_tiles * tile // 128
    pack = pl.pallas_call(
        functools.partial(kernel, npath),
        out_shape=pltpu.VMEM((2 * answer_lines + left_lines + 8, 128), F32),
        in_specs=[hbm] * 5,
        out_specs=vmem,
        scratch_shapes=[
            pltpu.VMEM((1, slots), jnp.int32),
            pltpu.VMEM((1, slots), jnp.int32),
            pltpu.SMEM((1,), jnp.int32),
            pltpu.VMEM((left_lines, 128), F32),
            pltpu.VMEM((slots, tile, tile), BF16),
            pltpu.VMEM((npath, 8, width), F32),
            pltpu.VMEM((2, npath, slots + 16, tile), BF16),
            pltpu.VMEM((2, 8, tile + 128), F32),
            pltpu.VMEM((2, 8, tile + 128), F32),
            pltpu.VMEM((npath, 8, 128), F32),
            pltpu.VMEM((2 * slots, tile), BF16),
            pltpu.VMEM((lines, width), BF16),
            pltpu.VMEM((slots // GROUP, GROUP, tile), F32),
            pltpu.VMEM((lines, tile), F32),
            pltpu.SemaphoreType.DMA((4,)),
            pltpu.SemaphoreType.DMA((slots // GROUP,)),
            pltpu.SemaphoreType.DMA((2, npath)),
            pltpu.SemaphoreType.DMA((2, 2, chunks + 1, npath)),
            pltpu.SemaphoreType.DMA((2, 2)),
            pltpu.SemaphoreType.DMA((2, npath)),
        ],
        compiler_params=pltpu.CompilerParams(
            collective_id=0, has_side_effects=True, vmem_limit_bytes=VMEM_LIMIT
        ),
        cost_estimate=pl.CostEstimate(
            flops=8 * 16 * slots * tile * tile,
            bytes_accessed=2 * slots * tile * tile,
            transcendentals=0,
        ),
    )(
        tiles,
        tile_rows.reshape(1, slots),
        tile_cols.reshape(1, slots),
        tile_counts,
        data.reshape(-1, 128),
    )
    answer, left = pl.pallas_call(
        unpack,
        out_shape=(
            jax.ShapeDtypeStruct((answer_lines, 128), F32),
            jax.ShapeDtypeStruct((left_lines, 128), F32),
        ),
        in_specs=[vmem],
        out_specs=(hbm, hbm),
        scratch_shapes=[pltpu.SemaphoreType.DMA((2,))],
    )(pack)
    left = left.reshape(-1)
    state = pack[answer_lines + left_lines + 8 :].reshape(CT_DEV, tile)
    last_right_step(
        tiles,
        tile_rows,
        tile_cols,
        tile_counts,
        left / jnp.sqrt(F32(row_tiles * tile * npath)),
        pack[answer_lines + left_lines, 0],
        state,
    )
    return answer.reshape(-1), left


def solution(mesh):
    placed = (
        P(("path", "mp"), None, None),
        P(("path", "mp")),
        P(("path", "mp")),
        P(("path", "mp")),
        P(("period", "path")),
    )
    return jax.shard_map(
        on_device,
        mesh=mesh,
        in_specs=placed,
        out_specs=(P(("period", "path", "mp")), P(("period", "path"))),
        check_vma=False,
    )
```

```python
import functools

import jax
import jax.numpy as jnp
from jax import lax
from jax.experimental import pallas as pl
from jax.experimental.pallas import tpu as pltpu
from jax.sharding import PartitionSpec as P

CT_DEV = 32
CHUNK = 16
GROUP = 8
VMEM_LIMIT = 56 * 1024 * 1024
F32 = jnp.float32
BF16 = jnp.bfloat16


def iota(shape, dim):
    return lax.broadcasted_iota(jnp.int32, shape, dim)


def total(x):
    return jnp.sum(jnp.sum(x, axis=0, keepdims=True), axis=1, keepdims=True)


def split(x):
    hi = x.astype(BF16).astype(F32)
    return hi, x - hi


def kernel(
    npath,
    tiles_hbm,
    rows_hbm,
    cols_hbm,
    counts_hbm,
    data_hbm,
    pack_ref,
    rows_ref,
    cols_ref,
    counts_ref,
    data_ref,
    tiles,
    info,
    terms,
    halves_out,
    halves_in,
    sums,
    picks,
    spread,
    prods,
    prior,
    small_sem,
    tile_sem,
    info_sem,
    term_sem,
    half_sem,
    sum_sem,
):
    slots, tile = tiles.shape[0], tiles.shape[1]
    groups, chunks = slots // GROUP, slots // CHUNK
    width = npath * slots
    cells = npath * CT_DEV
    me = lax.axis_index("path")
    mp = lax.axis_index("mp")

    def tile_copy(g):
        part = pl.ds(g * GROUP, GROUP)
        return pltpu.make_async_copy(tiles_hbm.at[part], tiles.at[part], tile_sem.at[g])

    def peer(step):
        return lax.rem(me + step, npath)

    def sender(step):
        return lax.rem(me + npath - step, npath)

    def to_peer(src, dst, sems, index, step, **other):
        return pltpu.make_async_remote_copy(
            src_ref=src,
            dst_ref=dst,
            send_sem=sems.at[(0, *index)],
            recv_sem=sems.at[(1, *index)],
            device_id={"path": peer(step), **other},
            device_id_type=pl.DeviceIdType.MESH,
        )

    smalls = [
        pltpu.make_async_copy(src, dst, small_sem.at[i])
        for i, (src, dst) in enumerate(
            (
                (data_hbm, data_ref),
                (rows_hbm, rows_ref),
                (cols_hbm, cols_ref),
                (counts_hbm, counts_ref),
            )
        )
    ]
    for copy in smalls:
        copy.start()
    for g in range(groups):
        tile_copy(g).start()

    barrier = pltpu.get_barrier_semaphore()
    for step in range(1, npath):
        for side in (mp, 1 - mp):
            pl.semaphore_signal(
                barrier,
                inc=1,
                device_id={"path": peer(step), "mp": side},
                device_id_type=pl.DeviceIdType.MESH,
            )
    pl.semaphore_signal(
        barrier, inc=1, device_id={"mp": 1 - mp}, device_id_type=pl.DeviceIdType.MESH
    )

    for copy in smalls:
        copy.wait()
    half_rows = data_ref.shape[0] // 2
    data = jnp.concatenate(
        [data_ref[pl.ds(0, half_rows, stride=2), :], data_ref[pl.ds(1, half_rows, stride=2), :]],
        axis=1,
    )
    live = iota((1, slots), 1) < counts_ref[0]
    row_code = jnp.where(live, rows_ref[...], -1).astype(F32)
    col_live = jnp.where(live, cols_ref[...], -1).astype(F32)

    diag = iota((slots, slots), 0) == iota((slots, slots), 1)
    col_down = jnp.sum(jnp.where(diag, col_live, 0.0), axis=1, keepdims=True)
    here = iota((slots, width), 1) - me * slots == iota((slots, width), 0)
    placed = jnp.sum(jnp.where(here, col_down, 0.0), axis=0, keepdims=True)
    line = iota((8, width), 0)
    info[me] = jnp.where(line == 0, placed, jnp.where(line == 1, total(data * data), 0.0))

    pl.semaphore_wait(barrier, 2 * npath - 1)

    def info_copy(step):
        return to_peer(info.at[me], info.at[me], info_sem, (step,), step)

    for step in range(1, npath):
        info_copy(step).start()

    q = iota((2 * slots, slots), 0)
    slot_of_q = q // 16 * 8 + q % 8
    row_q = jnp.sum(
        jnp.where(slot_of_q == iota((2 * slots, slots), 1), row_code, 0.0), axis=1, keepdims=True
    )
    qc = iota((2 * slots, 16), 0)
    offset = (qc % 16 // 8 * 8).astype(F32)
    pick_rows = ((row_q + offset == iota((2 * slots, 16), 1).astype(F32)) & (row_q >= 0)).astype(BF16)

    row_down = jnp.sum(jnp.where(diag, row_code, 0.0), axis=1, keepdims=True)
    q = iota((slots, 2 * slots), 1)
    slot_of_q = q // 16 * 8 + q % 8
    row_q = jnp.sum(
        jnp.where(slot_of_q == iota((slots, 2 * slots), 0), row_down, 0.0), axis=0, keepdims=True
    )
    offset = (iota((16, 2 * slots), 1) % 16 // 8 * 8).astype(F32)
    sum_rows = (
        (row_q + offset == iota((16, 2 * slots), 0).astype(F32)) & (row_q >= 0)
    ).astype(BF16)

    def term_copy(which, chunk, step):
        part = pl.ds(chunk * CHUNK, CHUNK)
        ref = terms.at[which, me, part]
        return to_peer(ref, ref, term_sem, (which, chunk, step), step)

    def norm_copy(step):
        ref = terms.at[1, me, pl.ds(slots, 16)]
        return to_peer(ref, ref, term_sem, (1, chunks, step), step)

    def fan_out(block):
        spot = iota((16, tile), 0) % 8
        rows = [jnp.where(spot == k, block, 0.0).astype(BF16) for k in range(GROUP)]
        return jnp.concatenate(rows, axis=1)

    def backward(which, left):
        hi, lo = split(left)
        both = jnp.concatenate([hi, lo], axis=0).astype(BF16)
        picks[...] = jnp.dot(pick_rows, both, preferred_element_type=F32).astype(BF16)

        def one_chunk(chunk, carry):
            parts = []
            for half in range(CHUNK // GROUP):
                g = chunk * (CHUNK // GROUP) + half
                if which == 0:
                    tile_copy(g).wait()
                block = picks[pl.ds(pl.multiple_of(g * 16, 16), 16), :].astype(F32)
                acc = jnp.dot(
                    fan_out(block),
                    tiles[pl.ds(g * GROUP, GROUP)].reshape(GROUP * tile, tile),
                    preferred_element_type=F32,
                )
                parts.append(acc[:8] + acc[8:])
            start = pl.multiple_of(chunk * CHUNK, CHUNK)
            terms[which, me, pl.ds(start, CHUNK), :] = jnp.concatenate(parts, axis=0).astype(BF16)
            for step in range(1, npath):
                term_copy(which, chunk, step).start()
            return carry

        lax.fori_loop(0, chunks, one_chunk, 0)

    def wait_terms(which):
        for chunk in range(chunks):
            for step in range(1, npath):
                term_copy(which, chunk, step).wait()

    def gathered(which):
        block = terms[which, :, :slots, :].reshape(width, tile)
        return jnp.dot(spread[...], block, preferred_element_type=F32)

    def sum_copy(step, far):
        ref = sums.at[me, mp]
        side = 1 - mp if far else mp
        return to_peer(ref, ref, sum_sem, (far, step), step, mp=side)

    def forward(which, right):
        hi, lo = split(right[:slots].reshape(groups, GROUP, tile))
        both = jnp.concatenate([hi, lo], axis=1)
        picks[...] = both.reshape(2 * slots, tile).astype(BF16)

        def two_groups(pair, carry):
            for half in range(2):
                g = pair * 2 + half
                block = picks[pl.ds(pl.multiple_of(g * 16, 16), 16), :].astype(F32)
                wide = fan_out(block)
                acc = jnp.zeros((16, tile), F32)
                for k in range(GROUP):
                    acc = acc + lax.dot_general(
                        wide[:, k * tile : k * tile + tile],
                        tiles[g * GROUP + k],
                        (((1,), (1,)), ((), ())),
                        preferred_element_type=F32,
                    )
                prods[g] = acc[:8] + acc[8:]
            return carry

        lax.fori_loop(0, groups // 2, two_groups, 0)
        hi, lo = split(prods[...])
        both = jnp.concatenate([hi, lo], axis=1).reshape(2 * slots, tile).astype(BF16)
        acc = jnp.dot(sum_rows, both, preferred_element_type=F32)
        rest = right[slots:]
        mine = acc[:8] + acc[8:]
        norm = jnp.broadcast_to(total(rest * rest), (8, 128))
        halves_out[which] = jnp.concatenate([mine, norm], axis=1)
        copy = pltpu.make_async_remote_copy(
            src_ref=halves_out.at[which],
            dst_ref=halves_in.at[which],
            send_sem=half_sem.at[0, which],
            recv_sem=half_sem.at[1, which],
            device_id={"mp": 1 - mp},
            device_id_type=pl.DeviceIdType.MESH,
        )
        copy.start()
        if which == 1:
            sums[me, mp] = jnp.concatenate([mine[:, :128], mine[:, 128:]], axis=0).astype(BF16)
            for step in range(1, npath):
                for far in range(2):
                    sum_copy(step, far).start()
        copy.wait()
        both = halves_out[which] + halves_in[which]
        return both[:, :tile], jnp.sqrt(both[:1, tile : tile + 1] + 1e-12)

    backward(0, data)

    for step in range(1, npath):
        info_copy(step).wait()
    facts = info[0]
    for p in range(1, npath):
        facts = facts + info[p]
    all_cols = facts[:1]
    beta0 = jnp.sqrt(facts[1:2, :1] + 1e-12)

    col_all_down = jnp.sum(
        jnp.where(diag, cols_ref[...].astype(F32), 0.0), axis=1, keepdims=True
    )
    spread[:slots] = (col_all_down == all_cols).astype(BF16)
    spread[slots:] = (iota((cells, width), 0).astype(F32) == all_cols).astype(BF16)

    wait_terms(0)
    right = gathered(0) / beta0
    prior[...] = right
    product, alpha0 = forward(0, right)
    left0 = data / beta0
    left = product / alpha0 - alpha0 * left0
    terms[1, me, slots:, :] = jnp.concatenate(split(left), axis=0).astype(BF16)
    for step in range(1, npath):
        norm_copy(step).start()
    backward(1, left)
    for step in range(1, npath):
        norm_copy(step).wait()
    lefts = terms[1, :, slots:, :].astype(F32)
    lefts = lefts[:, :8] + lefts[:, 8:]
    beta1 = jnp.sqrt(total(jnp.sum(lefts * lefts, axis=0)) + 1e-12)
    left = left / beta1
    wait_terms(1)
    right = gathered(1) / beta1 - (beta1 / alpha0) * prior[...]
    own = pl.ds(slots + me * CT_DEV, CT_DEV)
    search = prior[own, :] / alpha0
    prior[...] = right
    product, alpha1 = forward(1, right)
    left = product / alpha1 - alpha1 * left
    state = prior[own, :] / alpha1
    rho = jnp.sqrt(alpha0 * alpha0 + beta1 * beta1)
    cosine, sine = alpha0 / rho, beta1 / rho
    theta = sine * alpha1
    rhobar = -cosine * alpha1
    phi = cosine * beta0
    phibar = sine * beta0
    first = phi / rho * search
    search = state - theta / rho * search

    def keep(block, base):
        for h in range(2):
            pack_ref[pl.ds(base + h, block.shape[0], stride=2), :] = block[:, h * 128 : h * 128 + 128]

    cells_end = 2 * CT_DEV
    rows_end = cells_end + 2 * half_rows
    keep(state, rows_end + 8)

    for step in range(1, npath):
        for far in range(2):
            sum_copy(step, far).wait()
    norm = total(left * left)
    for step in range(1, npath):
        p = sender(step)
        whole = sums[p, 0].astype(F32) + sums[p, 1].astype(F32)
        kept = terms[1, p, slots:, :].astype(F32)
        kept = (kept[:8] + kept[8:]) / beta1
        kept = jnp.concatenate([kept[:, :128], kept[:, 128:]], axis=0)
        whole = whole / alpha1 - alpha1 * kept
        norm = norm + total(whole * whole)
    beta2 = jnp.sqrt(norm + 1e-12)
    left = left / beta2 * jnp.sqrt(F32(npath * half_rows * tile))
    rho = jnp.sqrt(rhobar * rhobar + beta2 * beta2)
    phi = rhobar / rho * phibar
    answer = first + phi / rho * search
    keep(answer, 0)
    keep(left, cells_end)
    pack_ref[rows_end : rows_end + 8] = jnp.broadcast_to(beta2, (8, 128))


def last_right_step(tiles, tile_rows, tile_cols, tile_counts, left, beta, state):
    slots, tile = tiles.shape[0], tiles.shape[1]
    npath = lax.axis_size("path")
    live = lax.iota(jnp.int32, slots) < tile_counts[0]
    picked = left.reshape(-1, tile).astype(BF16)[tile_rows]
    prods = jnp.einsum("sij,si->sj", tiles, picked, preferred_element_type=F32)
    place = (lax.iota(jnp.int32, npath * CT_DEV)[:, None] == tile_cols[None, :]) & live[None, :]
    cells = jnp.dot(place.astype(F32), prods, precision=lax.Precision.HIGHEST)
    own = lax.psum_scatter(cells, "path", scatter_dimension=0, tiled=True) - beta * state
    alpha = jnp.sqrt(lax.psum(jnp.sum(own * own), ("path", "mp")) + 1e-12)
    return own / alpha, alpha


def on_device(tiles, tile_rows, tile_cols, tile_counts, data):
    slots, tile = tiles.shape[0], tiles.shape[1]
    npath = lax.axis_size("path")
    row_tiles = data.shape[0] // tile
    width, lines = npath * slots, slots + npath * CT_DEV
    chunks = slots // CHUNK
    hbm = pl.BlockSpec(memory_space=pltpu.HBM)
    vmem = pl.BlockSpec(memory_space=pltpu.VMEM)
    answer_lines, left_lines = CT_DEV * tile // 128, row_tiles * tile // 128
    pack = pl.pallas_call(
        functools.partial(kernel, npath),
        out_shape=pltpu.VMEM((2 * answer_lines + left_lines + 8, 128), F32),
        in_specs=[hbm] * 5,
        out_specs=vmem,
        scratch_shapes=[
            pltpu.VMEM((1, slots), jnp.int32),
            pltpu.VMEM((1, slots), jnp.int32),
            pltpu.SMEM((1,), jnp.int32),
            pltpu.VMEM((left_lines, 128), F32),
            pltpu.VMEM((slots, tile, tile), BF16),
            pltpu.VMEM((npath, 8, width), F32),
            pltpu.VMEM((2, npath, slots + 16, tile), BF16),
            pltpu.VMEM((2, 8, tile + 128), F32),
            pltpu.VMEM((2, 8, tile + 128), F32),
            pltpu.VMEM((npath, 2, 16, 128), BF16),
            pltpu.VMEM((2 * slots, tile), BF16),
            pltpu.VMEM((lines, width), BF16),
            pltpu.VMEM((slots // GROUP, GROUP, tile), F32),
            pltpu.VMEM((lines, tile), F32),
            pltpu.SemaphoreType.DMA((4,)),
            pltpu.SemaphoreType.DMA((slots // GROUP,)),
            pltpu.SemaphoreType.DMA((2, npath)),
            pltpu.SemaphoreType.DMA((2, 2, chunks + 1, npath)),
            pltpu.SemaphoreType.DMA((2, 2)),
            pltpu.SemaphoreType.DMA((2, 2, npath)),
        ],
        compiler_params=pltpu.CompilerParams(
            collective_id=0, has_side_effects=True, vmem_limit_bytes=VMEM_LIMIT
        ),
        cost_estimate=pl.CostEstimate(
            flops=8 * 16 * slots * tile * tile,
            bytes_accessed=2 * slots * tile * tile,
            transcendentals=0,
        ),
    )(
        tiles,
        tile_rows.reshape(1, slots),
        tile_cols.reshape(1, slots),
        tile_counts,
        data.reshape(-1, 128),
    )
    answer = pack[:answer_lines]
    left = pack[answer_lines : answer_lines + left_lines].reshape(-1)
    rest = pack[answer_lines + left_lines :]
    last_right_step(
        tiles,
        tile_rows,
        tile_cols,
        tile_counts,
        left / jnp.sqrt(F32(row_tiles * tile * npath)),
        rest[0, 0],
        rest[8:].reshape(CT_DEV, tile),
    )
    return answer.reshape(-1), left


def solution(mesh):
    placed = (
        P(("path", "mp"), None, None),
        P(("path", "mp")),
        P(("path", "mp")),
        P(("path", "mp")),
        P(("period", "path")),
    )
    return jax.shard_map(
        on_device,
        mesh=mesh,
        in_specs=placed,
        out_specs=(P(("period", "path", "mp")), P(("period", "path"))),
        check_vma=False,
    )
```

```python
import functools

import jax
import jax.numpy as jnp
from jax import lax
from jax.experimental import pallas as pl
from jax.experimental.pallas import tpu as pltpu
from jax.sharding import PartitionSpec as P

CT_DEV = 32
CHUNK = 16
GROUP = 8
VMEM_LIMIT = 56 * 1024 * 1024
F32 = jnp.float32
BF16 = jnp.bfloat16


def iota(shape, dim):
    return lax.broadcasted_iota(jnp.int32, shape, dim)


def total(x):
    return jnp.sum(jnp.sum(x, axis=0, keepdims=True), axis=1, keepdims=True)


def split(x):
    hi = x.astype(BF16).astype(F32)
    return hi, x - hi


def kernel(
    npath,
    tiles_hbm,
    rows_hbm,
    cols_hbm,
    counts_hbm,
    data_hbm,
    pack_ref,
    rows_ref,
    cols_ref,
    counts_ref,
    data_ref,
    tiles,
    info,
    terms,
    halves_out,
    halves_in,
    sums,
    picks,
    spread,
    prods,
    prior,
    small_sem,
    tile_sem,
    info_sem,
    term_sem,
    half_sem,
    sum_sem,
):
    slots, tile = tiles.shape[0], tiles.shape[1]
    groups, chunks = slots // GROUP, slots // CHUNK
    width = npath * slots
    cells = npath * CT_DEV
    me = lax.axis_index("path")
    mp = lax.axis_index("mp")

    def tile_copy(g):
        part = pl.ds(g * GROUP, GROUP)
        return pltpu.make_async_copy(tiles_hbm.at[part], tiles.at[part], tile_sem.at[g])

    def peer(step):
        return lax.rem(me + step, npath)

    def sender(step):
        return lax.rem(me + npath - step, npath)

    def to_peer(src, dst, sems, index, step, **other):
        return pltpu.make_async_remote_copy(
            src_ref=src,
            dst_ref=dst,
            send_sem=sems.at[(0, *index)],
            recv_sem=sems.at[(1, *index)],
            device_id={"path": peer(step), **other},
            device_id_type=pl.DeviceIdType.MESH,
        )

    smalls = [
        pltpu.make_async_copy(src, dst, small_sem.at[i])
        for i, (src, dst) in enumerate(
            (
                (data_hbm, data_ref),
                (rows_hbm, rows_ref),
                (cols_hbm, cols_ref),
                (counts_hbm, counts_ref),
            )
        )
    ]
    for copy in smalls:
        copy.start()
    for g in range(groups):
        tile_copy(g).start()

    barrier = pltpu.get_barrier_semaphore()
    for step in range(1, npath):
        for side in (mp, 1 - mp):
            pl.semaphore_signal(
                barrier,
                inc=1,
                device_id={"path": peer(step), "mp": side},
                device_id_type=pl.DeviceIdType.MESH,
            )
    pl.semaphore_signal(
        barrier, inc=1, device_id={"mp": 1 - mp}, device_id_type=pl.DeviceIdType.MESH
    )

    for copy in smalls:
        copy.wait()
    half_rows = data_ref.shape[0] // 2
    data = jnp.concatenate(
        [data_ref[pl.ds(0, half_rows, stride=2), :], data_ref[pl.ds(1, half_rows, stride=2), :]],
        axis=1,
    )
    live = iota((1, slots), 1) < counts_ref[0]
    row_code = jnp.where(live, rows_ref[...], -1).astype(F32)
    col_live = jnp.where(live, cols_ref[...], -1).astype(F32)

    diag = iota((slots, slots), 0) == iota((slots, slots), 1)
    col_down = jnp.sum(jnp.where(diag, col_live, 0.0), axis=1, keepdims=True)
    here = iota((slots, width), 1) - me * slots == iota((slots, width), 0)
    placed = jnp.sum(jnp.where(here, col_down, 0.0), axis=0, keepdims=True)
    line = iota((8, width), 0)
    info[me] = jnp.where(line == 0, placed, jnp.where(line == 1, total(data * data), 0.0))

    pl.semaphore_wait(barrier, 2 * npath - 1)

    def info_copy(step):
        return to_peer(info.at[me], info.at[me], info_sem, (step,), step)

    for step in range(1, npath):
        info_copy(step).start()

    q = iota((2 * slots, slots), 0)
    slot_of_q = q // 16 * 8 + q % 8
    row_q = jnp.sum(
        jnp.where(slot_of_q == iota((2 * slots, slots), 1), row_code, 0.0), axis=1, keepdims=True
    )
    qc = iota((2 * slots, 16), 0)
    offset = (qc % 16 // 8 * 8).astype(F32)
    pick_rows = ((row_q + offset == iota((2 * slots, 16), 1).astype(F32)) & (row_q >= 0)).astype(BF16)

    row_down = jnp.sum(jnp.where(diag, row_code, 0.0), axis=1, keepdims=True)
    q = iota((slots, 2 * slots), 1)
    slot_of_q = q // 16 * 8 + q % 8
    row_q = jnp.sum(
        jnp.where(slot_of_q == iota((slots, 2 * slots), 0), row_down, 0.0), axis=0, keepdims=True
    )
    offset = (iota((16, 2 * slots), 1) % 16 // 8 * 8).astype(F32)
    sum_rows = (
        (row_q + offset == iota((16, 2 * slots), 0).astype(F32)) & (row_q >= 0)
    ).astype(BF16)

    def term_copy(which, chunk, step):
        part = pl.ds(chunk * CHUNK, CHUNK)
        ref = terms.at[which, me, part]
        return to_peer(ref, ref, term_sem, (which, chunk, step), step)

    def norm_copy(step):
        ref = terms.at[1, me, pl.ds(slots, 16)]
        return to_peer(ref, ref, term_sem, (1, chunks, step), step)

    def fan_out(block):
        spot = iota((16, tile), 0) % 8
        rows = [jnp.where(spot == k, block, 0.0).astype(BF16) for k in range(GROUP)]
        return jnp.concatenate(rows, axis=1)

    def backward(which, left):
        hi, lo = split(left)
        both = jnp.concatenate([hi, lo], axis=0).astype(BF16)
        picks[...] = jnp.dot(pick_rows, both, preferred_element_type=F32).astype(BF16)

        def one_chunk(chunk, carry):
            parts = []
            for half in range(CHUNK // GROUP):
                g = chunk * (CHUNK // GROUP) + half
                if which == 0:
                    tile_copy(g).wait()
                block = picks[pl.ds(pl.multiple_of(g * 16, 16), 16), :].astype(F32)
                acc = jnp.dot(
                    fan_out(block),
                    tiles[pl.ds(g * GROUP, GROUP)].reshape(GROUP * tile, tile),
                    preferred_element_type=F32,
                )
                parts.append(acc[:8] + acc[8:])
            start = pl.multiple_of(chunk * CHUNK, CHUNK)
            terms[which, me, pl.ds(start, CHUNK), :] = jnp.concatenate(parts, axis=0).astype(BF16)
            for step in range(1, npath):
                term_copy(which, chunk, step).start()
            return carry

        lax.fori_loop(0, chunks, one_chunk, 0, unroll=2)

    def wait_terms(which):
        for chunk in range(chunks):
            for step in range(1, npath):
                term_copy(which, chunk, step).wait()

    def gathered(which):
        block = terms[which, :, :slots, :].reshape(width, tile)
        return jnp.dot(spread[...], block, preferred_element_type=F32)

    def sum_copy(step, far):
        ref = sums.at[me, mp]
        side = 1 - mp if far else mp
        return to_peer(ref, ref, sum_sem, (far, step), step, mp=side)

    def forward(which, right):
        hi, lo = split(right[:slots].reshape(groups, GROUP, tile))
        both = jnp.concatenate([hi, lo], axis=1)
        picks[...] = both.reshape(2 * slots, tile).astype(BF16)

        def two_groups(pair, carry):
            for half in range(2):
                g = pair * 2 + half
                block = picks[pl.ds(pl.multiple_of(g * 16, 16), 16), :].astype(F32)
                wide = fan_out(block)
                acc = jnp.zeros((16, tile), F32)
                for k in range(GROUP):
                    acc = acc + lax.dot_general(
                        wide[:, k * tile : k * tile + tile],
                        tiles[g * GROUP + k],
                        (((1,), (1,)), ((), ())),
                        preferred_element_type=F32,
                    )
                prods[g] = acc[:8] + acc[8:]
            return carry

        lax.fori_loop(0, groups // 2, two_groups, 0, unroll=2)
        hi, lo = split(prods[...])
        both = jnp.concatenate([hi, lo], axis=1).reshape(2 * slots, tile).astype(BF16)
        acc = jnp.dot(sum_rows, both, preferred_element_type=F32)
        rest = right[slots:]
        mine = acc[:8] + acc[8:]
        norm = jnp.broadcast_to(total(rest * rest), (8, 128))
        halves_out[which] = jnp.concatenate([mine, norm], axis=1)
        copy = pltpu.make_async_remote_copy(
            src_ref=halves_out.at[which],
            dst_ref=halves_in.at[which],
            send_sem=half_sem.at[0, which],
            recv_sem=half_sem.at[1, which],
            device_id={"mp": 1 - mp},
            device_id_type=pl.DeviceIdType.MESH,
        )
        copy.start()
        if which == 1:
            sums[me, mp] = jnp.concatenate([mine[:, :128], mine[:, 128:]], axis=0).astype(BF16)
            for step in range(1, npath):
                for far in range(2):
                    sum_copy(step, far).start()
        copy.wait()
        both = halves_out[which] + halves_in[which]
        return both[:, :tile], jnp.sqrt(both[:1, tile : tile + 1] + 1e-12)

    backward(0, data)

    for step in range(1, npath):
        info_copy(step).wait()
    facts = info[0]
    for p in range(1, npath):
        facts = facts + info[p]
    all_cols = facts[:1]
    beta0 = jnp.sqrt(facts[1:2, :1] + 1e-12)

    col_all_down = jnp.sum(
        jnp.where(diag, cols_ref[...].astype(F32), 0.0), axis=1, keepdims=True
    )
    spread[:slots] = (col_all_down == all_cols).astype(BF16)
    spread[slots:] = (iota((cells, width), 0).astype(F32) == all_cols).astype(BF16)

    wait_terms(0)
    right = gathered(0) / beta0
    prior[...] = right
    product, alpha0 = forward(0, right)
    left0 = data / beta0
    left = product / alpha0 - alpha0 * left0
    terms[1, me, slots:, :] = jnp.concatenate(split(left), axis=0).astype(BF16)
    for step in range(1, npath):
        norm_copy(step).start()
    backward(1, left)
    for step in range(1, npath):
        norm_copy(step).wait()
    lefts = terms[1, :, slots:, :].astype(F32)
    lefts = lefts[:, :8] + lefts[:, 8:]
    beta1 = jnp.sqrt(total(jnp.sum(lefts * lefts, axis=0)) + 1e-12)
    left = left / beta1
    wait_terms(1)
    right = gathered(1) / beta1 - (beta1 / alpha0) * prior[...]
    own = pl.ds(slots + me * CT_DEV, CT_DEV)
    search = prior[own, :] / alpha0
    prior[...] = right
    product, alpha1 = forward(1, right)
    left = product / alpha1 - alpha1 * left
    state = prior[own, :] / alpha1
    rho = jnp.sqrt(alpha0 * alpha0 + beta1 * beta1)
    cosine, sine = alpha0 / rho, beta1 / rho
    theta = sine * alpha1
    rhobar = -cosine * alpha1
    phi = cosine * beta0
    phibar = sine * beta0
    first = phi / rho * search
    search = state - theta / rho * search

    def keep(block, base):
        for h in range(2):
            pack_ref[pl.ds(base + h, block.shape[0], stride=2), :] = block[:, h * 128 : h * 128 + 128]

    cells_end = 2 * CT_DEV
    rows_end = cells_end + 2 * half_rows
    keep(state, rows_end + 8)

    for step in range(1, npath):
        for far in range(2):
            sum_copy(step, far).wait()
    norm = total(left * left)
    for step in range(1, npath):
        p = sender(step)
        whole = sums[p, 0].astype(F32) + sums[p, 1].astype(F32)
        kept = terms[1, p, slots:, :].astype(F32)
        kept = (kept[:8] + kept[8:]) / beta1
        kept = jnp.concatenate([kept[:, :128], kept[:, 128:]], axis=0)
        whole = whole / alpha1 - alpha1 * kept
        norm = norm + total(whole * whole)
    beta2 = jnp.sqrt(norm + 1e-12)
    left = left / beta2 * jnp.sqrt(F32(npath * half_rows * tile))
    rho = jnp.sqrt(rhobar * rhobar + beta2 * beta2)
    phi = rhobar / rho * phibar
    answer = first + phi / rho * search
    keep(answer, 0)
    keep(left, cells_end)
    pack_ref[rows_end : rows_end + 8] = jnp.broadcast_to(beta2, (8, 128))


def last_right_step(tiles, tile_rows, tile_cols, tile_counts, left, beta, state):
    slots, tile = tiles.shape[0], tiles.shape[1]
    npath = lax.axis_size("path")
    live = lax.iota(jnp.int32, slots) < tile_counts[0]
    picked = left.reshape(-1, tile).astype(BF16)[tile_rows]
    prods = jnp.einsum("sij,si->sj", tiles, picked, preferred_element_type=F32)
    place = (lax.iota(jnp.int32, npath * CT_DEV)[:, None] == tile_cols[None, :]) & live[None, :]
    cells = jnp.dot(place.astype(F32), prods, precision=lax.Precision.HIGHEST)
    own = lax.psum_scatter(cells, "path", scatter_dimension=0, tiled=True) - beta * state
    alpha = jnp.sqrt(lax.psum(jnp.sum(own * own), ("path", "mp")) + 1e-12)
    return own / alpha, alpha


def on_device(tiles, tile_rows, tile_cols, tile_counts, data):
    slots, tile = tiles.shape[0], tiles.shape[1]
    npath = lax.axis_size("path")
    row_tiles = data.shape[0] // tile
    width, lines = npath * slots, slots + npath * CT_DEV
    chunks = slots // CHUNK
    hbm = pl.BlockSpec(memory_space=pltpu.HBM)
    vmem = pl.BlockSpec(memory_space=pltpu.VMEM)
    answer_lines, left_lines = CT_DEV * tile // 128, row_tiles * tile // 128
    pack = pl.pallas_call(
        functools.partial(kernel, npath),
        out_shape=pltpu.VMEM((2 * answer_lines + left_lines + 8, 128), F32),
        in_specs=[hbm] * 5,
        out_specs=vmem,
        scratch_shapes=[
            pltpu.VMEM((1, slots), jnp.int32),
            pltpu.VMEM((1, slots), jnp.int32),
            pltpu.SMEM((1,), jnp.int32),
            pltpu.VMEM((left_lines, 128), F32),
            pltpu.VMEM((slots, tile, tile), BF16),
            pltpu.VMEM((npath, 8, width), F32),
            pltpu.VMEM((2, npath, slots + 16, tile), BF16),
            pltpu.VMEM((2, 8, tile + 128), F32),
            pltpu.VMEM((2, 8, tile + 128), F32),
            pltpu.VMEM((npath, 2, 16, 128), BF16),
            pltpu.VMEM((2 * slots, tile), BF16),
            pltpu.VMEM((lines, width), BF16),
            pltpu.VMEM((slots // GROUP, GROUP, tile), F32),
            pltpu.VMEM((lines, tile), F32),
            pltpu.SemaphoreType.DMA((4,)),
            pltpu.SemaphoreType.DMA((slots // GROUP,)),
            pltpu.SemaphoreType.DMA((2, npath)),
            pltpu.SemaphoreType.DMA((2, 2, chunks + 1, npath)),
            pltpu.SemaphoreType.DMA((2, 2)),
            pltpu.SemaphoreType.DMA((2, 2, npath)),
        ],
        compiler_params=pltpu.CompilerParams(
            collective_id=0, has_side_effects=True, vmem_limit_bytes=VMEM_LIMIT
        ),
        cost_estimate=pl.CostEstimate(
            flops=8 * 16 * slots * tile * tile,
            bytes_accessed=2 * slots * tile * tile,
            transcendentals=0,
        ),
    )(
        tiles,
        tile_rows.reshape(1, slots),
        tile_cols.reshape(1, slots),
        tile_counts,
        data.reshape(-1, 128),
    )
    answer = pack[:answer_lines]
    left = pack[answer_lines : answer_lines + left_lines].reshape(-1)
    rest = pack[answer_lines + left_lines :]
    last_right_step(
        tiles,
        tile_rows,
        tile_cols,
        tile_counts,
        left / jnp.sqrt(F32(row_tiles * tile * npath)),
        rest[0, 0],
        rest[8:].reshape(CT_DEV, tile),
    )
    return answer.reshape(-1), left


def solution(mesh):
    placed = (
        P(("path", "mp"), None, None),
        P(("path", "mp")),
        P(("path", "mp")),
        P(("path", "mp")),
        P(("period", "path")),
    )
    return jax.shard_map(
        on_device,
        mesh=mesh,
        in_specs=placed,
        out_specs=(P(("period", "path", "mp")), P(("period", "path"))),
        check_vma=False,
    )
```
